32 devices in a mesh: az: 8 (over y, x, core), rad: 4 (over z).
Axes of the slice: x: 2, y: 2, z: 4, core: 2. Of those that a mesh axis runs over, the one named last changes fastest.
Arguments:
- block_mass: float32 [8, 4, 512, 128], P('az', 'rad'), may hold values from 0.5 to 4
- block_flux: float32 [8, 4, 512, 9, 128], P('az', 'rad'), may hold values from -6 to 6
- block_dest: int32 [8, 4, 512], P('az', 'rad'), may hold values from 0 to 2047, as said below
- block_count: int32 [8, 4], P('az', 'rad'), may hold values from 128 to 512, as said below
Outputs:
- smoothed: float32 [10, 64, 32, 512], P(None, 'az', None, 'rad')
- force: float32 [3, 64, 32, 512], P(None, 'az', None, 'rad')
- strain: float32 [6, 64, 32, 512], P(None, 'az', None, 'rad')
The draws below stay inside these ranges and needn't reach their ends.
Inputs may be any that keep to these rules, and one draw needn't show every extreme that they name: `block_dest`: the azimuthal row of a block of device (a, b) lies from 2 rows before to 2 rows after the rows a * 8 to a * 8 + 7, cyclically over 64 rows. `block_count`: some device is full in every draw.
All inputs are finite; a program needn't handle non-finite values.
Results may differ from the reference program's by a relative error of at most 0.000076.
Values sent between devices are 32-bit elements; how exact they have to be, the bound alone decides.
A program may use at most 64 MiB of HBM per device.

```python
import math
import jax
import jax.numpy as jnp

CA = 8
H = 32
CR = 128
SLOTS = 512
NA = 64
NR = 512
N_AZ = 8
N_RAD = 4


def draw_block_dest(key, part):
    first, second = jax.random.split(key)
    offset_rows = jax.random.randint(first, (N_AZ, N_RAD, SLOTS), -2, CA + 2)
    height_cell = jax.random.randint(second, (N_AZ, N_RAD, SLOTS), 0, H)
    offset_rows = offset_rows.at[0, 0, 0].set(-1).at[0, 0, 1].set(0)
    height_cell = height_cell.at[0, 0, 0].set(H - 1).at[0, 0, 1].set(0)
    sector_start = jnp.arange(N_AZ, dtype=jnp.int32)[:, None, None] * CA
    row_index = jnp.mod(sector_start + offset_rows, CA * N_AZ)
    return (row_index * H + height_cell).astype(jnp.int32)


def draw_block_count(key, part):
    first, second = jax.random.split(key)
    total = N_AZ * N_RAD
    counts = jax.random.randint(first, (total,), SLOTS // 4, SLOTS + 1)
    chosen = jax.random.randint(second, (), 0, total)
    device_ids = jnp.arange(total, dtype=jnp.int32)
    filled = jnp.where(device_ids == chosen, SLOTS, counts)
    filled = jnp.where(device_ids == jnp.mod(chosen + 1, total), SLOTS // 4, filled)
    return filled.reshape(N_AZ, N_RAD).astype(jnp.int32)


def steps_of(rng, dims, shards, least, high):
    factor_of = 1.0
    for dim, blocks in shards:
        draws = jax.random.uniform(jax.random.fold_in(jax.random.fold_in(rng, 6), dim), (blocks,), jnp.float32, least / len(shards), high / len(shards))
        factor_of = factor_of * jnp.repeat(jnp.exp(draws), dims[dim] // blocks).reshape((-1,) + (1,) * (len(dims) - 1 - dim))
    return factor_of


def bell_draw(rng, dims, width, reach, cuts=(), held_as=jnp.bfloat16):
    array = width * jax.random.normal(rng, dims, jnp.float32)
    if cuts:
        array = array * steps_of(rng, dims, cuts, -0.22, 0.18)
    return jnp.clip(array, -reach, reach).astype(held_as)


def setup_inputs(seed: int = 0) -> dict:
    seeds = jax.random.split(jax.random.key(seed), 5)
    block_mass = jnp.clip(jnp.exp(math.log(4.0) - 2.0794415 * jax.random.uniform(seeds[0], (N_AZ, N_RAD, SLOTS, CR), jnp.float32) ** steps_of(seeds[0], (N_AZ, N_RAD, SLOTS, CR), ((0, 8), (1, 4)), -0.2, 0.2)), 0.5, 4.0)
    block_flux = bell_draw(seeds[1], (N_AZ, N_RAD, SLOTS, 9, CR), 1.0, 6.0, ((0, 8), (1, 4)), jnp.float32)
    block_dest = draw_block_dest(jax.random.fold_in(seeds[4], 71), 0)
    block_count = draw_block_count(jax.random.fold_in(seeds[4], 71), 0)
    return dict(block_mass=block_mass, block_flux=block_flux, block_dest=block_dest, block_count=block_count)


density_base = 0.5


def smooth_grid(fields):
    fields = 0.25 * jnp.roll(fields, 1, 1) + 0.5 * fields + 0.25 * jnp.roll(fields, -1, 1)
    padded = jnp.pad(fields, ((0, 0), (0, 0), (0, 0), (1, 1)))
    fields = 0.25 * padded[..., :-2] + 0.5 * padded[..., 1:-1] + 0.25 * padded[..., 2:]
    padded = jnp.pad(fields, ((0, 0), (0, 0), (1, 1), (0, 0)))
    return 0.25 * padded[:, :, :-2] + 0.5 * padded[:, :, 1:-1] + 0.25 * padded[:, :, 2:]


def assemble(grad_az, grad_height, grad_rad, center, recip):
    force = jnp.stack([grad_az[3] + grad_height[6] + grad_rad[7] + 2.0 * center[7] * recip,
                       grad_az[6] + grad_height[4] + grad_rad[8],
                       grad_az[7] + grad_height[8] + grad_rad[5] + (center[5] - center[3]) * recip])
    strain = jnp.stack([grad_az[0] + center[2] * recip, grad_height[1], grad_rad[2],
                        0.5 * (grad_height[0] + grad_az[1]),
                        0.5 * (grad_rad[0] + grad_az[2] - center[0] * recip),
                        0.5 * (grad_rad[1] + grad_height[2])])
    return force, strain


def reference(block_mass, block_flux, block_dest, block_count):
    values = jnp.concatenate([block_mass[:, :, :, None, :], block_flux], axis=3)
    live = (jnp.arange(SLOTS, dtype=jnp.int32)[None, None, :] < block_count[:, :, None]).astype(jnp.float32)
    band_index = jnp.arange(N_RAD, dtype=jnp.int32)[None, :, None]
    target = (block_dest * N_RAD + band_index).astype(jnp.int32)
    summed = jax.ops.segment_sum((values * live[..., None, None]).reshape(-1, 10, CR),
                                 target.reshape(-1), num_segments=NA * H * N_RAD)
    fields = summed.reshape(NA, H, N_RAD, 10, CR).transpose(3, 0, 1, 2, 4).reshape(10, NA, H, NR)
    smoothed = smooth_grid(fields)
    velocity = smoothed[1:4] / (smoothed[0:1] + density_base)
    combined = jnp.concatenate([velocity, smoothed[4:]], axis=0)
    radius = NR + jnp.arange(NR, dtype=jnp.float32) + 0.5
    dtheta = 2.0 * math.pi / NA
    scale_az = 0.5 / (radius * dtheta)
    recip = 1.0 / radius
    grad_az = (jnp.roll(combined, -1, 1) - jnp.roll(combined, 1, 1)) * scale_az
    padded = jnp.pad(combined, ((0, 0), (0, 0), (0, 0), (1, 1)))
    grad_rad = (padded[..., 2:] - padded[..., :-2]) * 0.5
    padded = jnp.pad(combined, ((0, 0), (0, 0), (1, 1), (0, 0)))
    grad_height = (padded[:, :, 2:] - padded[:, :, :-2]) * 0.5
    force, strain = assemble(grad_az, grad_height, grad_rad, combined, recip)
    return smoothed, force, strain
```

```python
import functools
import math

import jax
import jax.numpy as jnp
from jax import lax
from jax.experimental import pallas as pl
from jax.experimental.pallas import tpu as pltpu
from jax.sharding import PartitionSpec as P

CA = 8
H = 32
CHANNELS = 10
ROWS = CA + 6
LINES = ROWS * H
SEND = 4 * H

density_base = 0.5

WIDE = (0, 1, 2, 3, 4, 7, 8)
ORDER = (0, 1, 2, 3, 4, 7, 8, 5, 6, 9)
FIRST = 4

MESH = pl.DeviceIdType.MESH


def split(value):
    high = value.astype(jnp.bfloat16)
    low = (value - high.astype(jnp.float32)).astype(jnp.bfloat16)
    return high, low


def kernel(
    n_az, n_rad, count_ref, dest_ref, mass_ref, flux_ref,
    smoothed_ref, force_ref, strain_ref,
    vin, high, low, weights, part, from_left, from_right,
    strip, strip_left, strip_right, edge_out, edge_left, edge_right,
    load_sem, send_sem, recv_sem, band_send, band_recv,
):
    sector = lax.axis_index("az")
    band = lax.axis_index("rad")
    slots = vin.shape[1]
    width = vin.shape[2]
    total_rows = CA * n_az
    right, left = lax.rem(sector + 1, n_az), lax.rem(sector + n_az - 1, n_az)
    outer, inner = band + 1, band - 1
    has_outer, has_inner = band < n_rad - 1, band > 0

    loads = []
    for c in range(CHANNELS):
        source = mass_ref if c == 0 else flux_ref.at[c - 1]
        copy = pltpu.make_async_copy(source, vin.at[c], load_sem.at[c])
        copy.start()
        loads.append(copy)

    barrier = pltpu.get_barrier_semaphore()
    for neighbour in (left, right):
        pl.semaphore_signal(barrier, inc=1, device_id={"az": neighbour}, device_id_type=MESH)

    @pl.when(has_outer)
    def _():
        pl.semaphore_signal(barrier, inc=1, device_id={"rad": outer}, device_id_type=MESH)

    @pl.when(has_inner)
    def _():
        pl.semaphore_signal(barrier, inc=1, device_id={"rad": inner}, device_id_type=MESH)

    dest = dest_ref[...]
    live = lax.broadcasted_iota(jnp.int32, (1, slots), 1) < count_ref[0, 0]
    height = dest & (H - 1)
    offset = (dest >> 5) - sector * CA + 2
    offset = jnp.where(offset < 0, offset + total_rows, offset)
    offset = jnp.where(offset >= total_rows, offset - total_rows, offset)
    apart = jnp.abs(lax.broadcasted_iota(jnp.int32, (H, slots), 0) - height)
    by_height = jnp.where(apart == 0, 0.5, jnp.where(apart == 1, 0.25, 0.0))
    for i in range(ROWS):
        apart = jnp.abs(i - 1 - offset)
        by_row = jnp.where(apart == 0, 0.5, jnp.where(apart == 1, 0.25, 0.0))
        by_row = jnp.where(live, by_row, 0.0)
        weights[i * H : (i + 1) * H, :] = (by_height * by_row).astype(jnp.bfloat16)

    depth = lax.broadcasted_iota(jnp.int32, (width, 128), 0)
    lane = lax.broadcasted_iota(jnp.int32, (width, 128), 1)
    place = lane // 20
    odd = lane % 2 == 1
    mirror = jnp.where(place == 1, jnp.where(odd, width - 2, 1), jnp.where(odd, width - 1, 0))
    mirror = jnp.where(place == 2, width - 1 - mirror, mirror)
    hit = (mirror == depth) & (place < 3)
    channel = (lane % 20) // 2
    select = jnp.concatenate(
        [jnp.where(hit & (channel == c), 1.0, 0.0).astype(jnp.bfloat16) for c in range(CHANNELS)],
        axis=0,
    )

    for c in range(CHANNELS):
        loads[c].wait()
        top, rest = split(vin[c])
        high[:, c * width : (c + 1) * width] = top
        low[:, c * width : (c + 1) * width] = rest

    def dot(a, b):
        return jnp.dot(a, b, preferred_element_type=jnp.float32)

    def deposited(top, rest):
        both = dot(weights[...], jnp.concatenate([top, rest], axis=1))
        return both[:, :128] + both[:, 128:]

    strip[...] = deposited(
        dot(high[...], select).astype(jnp.bfloat16), dot(low[...], select).astype(jnp.bfloat16)
    )

    pl.semaphore_wait(
        barrier, 2 + has_outer.astype(jnp.int32) + has_inner.astype(jnp.int32)
    )
    to_outer = pltpu.make_async_remote_copy(
        src_ref=strip, dst_ref=strip_left, send_sem=band_send.at[0], recv_sem=band_recv.at[0],
        device_id={"rad": outer}, device_id_type=MESH,
    )
    to_inner = pltpu.make_async_remote_copy(
        src_ref=strip, dst_ref=strip_right, send_sem=band_send.at[1], recv_sem=band_recv.at[1],
        device_id={"rad": inner}, device_id_type=MESH,
    )

    @pl.when(has_outer)
    def _():
        to_outer.start()

    @pl.when(has_inner)
    def _():
        to_inner.start()

    sends = {}

    def send(name, source_right, target_left, source_left, target_right):
        pair = []
        for way, (source, target, device) in enumerate(
            ((source_right, target_left, right), (source_left, target_right, left))
        ):
            copy = pltpu.make_async_remote_copy(
                src_ref=source, dst_ref=target,
                send_sem=send_sem.at[way, name], recv_sem=recv_sem.at[way, name],
                device_id={"az": device}, device_id_type=MESH,
            )
            copy.start()
            pair.append(copy)
        sends[name] = pair

    def deposit_and_send(c):
        columns = slice(c * width, (c + 1) * width)
        part[c] = deposited(high[:, columns], low[:, columns])
        wide = c in WIDE
        size = SEND if wide else SEND - H
        skip = 0 if wide else H
        send(
            c,
            part.at[c, pl.ds(LINES - size, size)], from_left.at[c, pl.ds(skip, size)],
            part.at[c, pl.ds(0, size)], from_right.at[c, pl.ds(0, size)],
        )

    for c in ORDER[:FIRST]:
        deposit_and_send(c)

    @pl.when(has_inner)
    def _():
        to_outer.wait_recv()

    @pl.when(jnp.logical_not(has_inner))
    def _():
        strip_left[...] = jnp.zeros_like(strip_left)

    @pl.when(has_outer)
    def _():
        to_inner.wait_recv()

    @pl.when(jnp.logical_not(has_outer))
    def _():
        strip_right[...] = jnp.zeros_like(strip_right)

    lane = lax.broadcasted_iota(jnp.int32, (LINES, 128), 1)
    beside = jnp.where(lane % 2 == 0, strip_right[...], strip_left[...])
    edges = jnp.where(lane < 40, beside, strip[...])
    edge_out[0] = jnp.transpose(edges[LINES - SEND :])[:64]
    edge_out[1] = jnp.transpose(edges[:SEND])[:64]
    send(CHANNELS, edge_out.at[0], edge_left, edge_out.at[1], edge_right)

    for c in ORDER[FIRST:]:
        deposit_and_send(c)

    def arrived(name):
        for copy in sends[name]:
            copy.wait_recv()

    arrived(CHANNELS)
    nothing = jnp.zeros((64, 128), jnp.float32)
    edges = jnp.concatenate(
        [
            edges[2 * H : 6 * H] + jnp.transpose(jnp.concatenate([edge_left[...], nothing], axis=0)),
            edges[6 * H : 8 * H],
            edges[8 * H : 12 * H] + jnp.transpose(jnp.concatenate([edge_right[...], nothing], axis=0)),
        ],
        axis=0,
    )
    lines = (CA + 2) * H
    lane = lax.broadcasted_iota(jnp.int32, (1, 128), 1)
    inside = jnp.where(lane % 2 == 0, has_outer.astype(jnp.float32), has_inner.astype(jnp.float32))
    edge_smoothed = 0.5 * edges + 0.25 * (pltpu.roll(edges, 108, 1) + pltpu.roll(edges, 88, 1))
    edge_smoothed = edge_smoothed * inside
    edge_combined = edge_smoothed[H : H + CA * H]
    density = 1.0 / (edge_combined + density_base)
    for c in (1, 2, 3):
        own = (lane == 2 * c) | (lane == 2 * c + 1)
        edge_combined = edge_combined * jnp.where(own, pltpu.roll(density, 2 * c, 1), 1.0)

    def beside_in_band(value, edge, c):
        edge = pltpu.roll(edge, 127 - 2 * c, 1)
        return (
            jnp.where(lane == 0, edge, pltpu.roll(value, 1, 1)),
            jnp.where(lane == 127, edge, pltpu.roll(value, 127, 1)),
        )

    radius = (width * n_rad + band * width + lane).astype(jnp.float32) + 0.5
    scale_az = 0.5 / (radius * (2.0 * math.pi / total_rows))
    recip = 1.0 / radius
    cell = lax.broadcasted_iota(jnp.int32, (CA * H, 1), 0) & (H - 1)

    def smooth(c):
        arrived(c)
        if c in WIDE:
            total = jnp.concatenate(
                [
                    part[c, 2 * H : 6 * H] + from_left[c],
                    part[c, 6 * H : 8 * H],
                    part[c, 8 * H : 12 * H] + from_right[c],
                ],
                axis=0,
            )
            edge = edges
        else:
            total = jnp.concatenate(
                [
                    part[c, 3 * H : 6 * H] + from_left[c, H:],
                    part[c, 6 * H : 8 * H],
                    part[c, 8 * H : 11 * H] + from_right[c, : 3 * H],
                ],
                axis=0,
            )
            edge = edges[H : H + CA * H]
        before, after = beside_in_band(total, edge, c)
        result = 0.5 * total + 0.25 * (before + after)
        smoothed_ref[c] = result[H : H + CA * H] if c in WIDE else result
        return result

    def grad_az(value):
        return (value[2 * H :] - value[: CA * H]) * scale_az

    def center(value):
        return value[H : H + CA * H]

    def grad_rad(value, c):
        before, after = beside_in_band(value, edge_combined, c)
        return (after - before) * 0.5

    def grad_height(value):
        below = jnp.where(cell == 0, 0.0, pltpu.roll(value, 1, 0))
        above = jnp.where(cell == H - 1, 0.0, pltpu.roll(value, CA * H - 1, 0))
        return (above - below) * 0.5

    density = 1.0 / (smooth(0) + density_base)
    value = smooth(1) * density
    middle = center(value)
    strain_ref[0] = grad_az(value)
    strain_ref[3] = grad_height(middle)
    strain_ref[4] = grad_rad(middle, 1) - middle * recip
    value = smooth(2) * density
    middle = center(value)
    strain_ref[1] = grad_height(middle)
    strain_ref[3] = 0.5 * (strain_ref[3] + grad_az(value))
    strain_ref[5] = grad_rad(middle, 2)
    value = smooth(3) * density
    middle = center(value)
    strain_ref[0] += middle * recip
    strain_ref[2] = grad_rad(middle, 3)
    strain_ref[4] = 0.5 * (strain_ref[4] + grad_az(value))
    strain_ref[5] = 0.5 * (strain_ref[5] + grad_height(middle))
    value = smooth(4)
    force_ref[0] = grad_az(value)
    force_ref[2] = -center(value) * recip
    value = smooth(7)
    force_ref[0] += grad_height(center(value))
    force_ref[1] = grad_az(value)
    value = smooth(8)
    middle = center(value)
    force_ref[0] += grad_rad(middle, 8) + 2.0 * middle * recip
    force_ref[2] += grad_az(value)
    force_ref[1] += grad_height(smooth(5))
    middle = smooth(6)
    force_ref[2] += grad_rad(middle, 6) + middle * recip
    middle = smooth(9)
    force_ref[1] += grad_rad(middle, 9)
    force_ref[2] += grad_height(middle)

    for pair in sends.values():
        for copy in pair:
            copy.wait_send()

    @pl.when(has_outer)
    def _():
        to_outer.wait_send()

    @pl.when(has_inner)
    def _():
        to_inner.wait_send()


def local(block_mass, block_flux, block_dest, block_count):
    n_az = lax.axis_size("az")
    n_rad = lax.axis_size("rad")
    slots, width = block_mass.shape[2:]
    cells = CA * H
    f32 = jnp.float32
    outs = pl.pallas_call(
        functools.partial(kernel, n_az, n_rad),
        out_shape=[jax.ShapeDtypeStruct((k, cells, width), f32) for k in (CHANNELS, 3, 6)],
        in_specs=[
            pl.BlockSpec(memory_space=pltpu.SMEM),
            pl.BlockSpec(memory_space=pltpu.VMEM),
            pl.BlockSpec(memory_space=pl.ANY),
            pl.BlockSpec(memory_space=pl.ANY),
        ],
        out_specs=[pl.BlockSpec(memory_space=pltpu.VMEM)] * 3,
        scratch_shapes=[
            pltpu.VMEM((CHANNELS, slots, width), f32),
            pltpu.VMEM((slots, CHANNELS * width), jnp.bfloat16),
            pltpu.VMEM((slots, CHANNELS * width), jnp.bfloat16),
            pltpu.VMEM((LINES, slots), jnp.bfloat16),
            pltpu.VMEM((CHANNELS, LINES, width), f32),
            pltpu.VMEM((CHANNELS, SEND, width), f32),
            pltpu.VMEM((CHANNELS, SEND, width), f32),
            pltpu.VMEM((LINES, 128), f32),
            pltpu.VMEM((LINES, 128), f32),
            pltpu.VMEM((LINES, 128), f32),
            pltpu.VMEM((2, 64, SEND), f32),
            pltpu.VMEM((64, SEND), f32),
            pltpu.VMEM((64, SEND), f32),
            pltpu.SemaphoreType.DMA((CHANNELS,)),
            pltpu.SemaphoreType.DMA((2, CHANNELS + 1)),
            pltpu.SemaphoreType.DMA((2, CHANNELS + 1)),
            pltpu.SemaphoreType.DMA((2,)),
            pltpu.SemaphoreType.DMA((2,)),
        ],
        compiler_params=pltpu.CompilerParams(
            collective_id=0, has_side_effects=True, vmem_limit_bytes=40 * 1024 * 1024
        ),
    )(
        block_count,
        block_dest.reshape(1, slots),
        block_mass.reshape(slots, width),
        jnp.transpose(block_flux.reshape(slots, 9, width), (1, 0, 2)),
    )
    return tuple(out.reshape(out.shape[0], CA, H, width) for out in outs)


def solution(mesh):
    return jax.shard_map(
        local,
        mesh=mesh,
        in_specs=(
            P("az", "rad", None, None),
            P("az", "rad", None, None, None),
            P("az", "rad", None),
            P("az", "rad"),
        ),
        out_specs=(
            P(None, "az", None, "rad"),
            P(None, "az", None, "rad"),
            P(None, "az", None, "rad"),
        ),
        check_vma=False,
    )
```

```python
import functools
import math

import jax
import jax.numpy as jnp
from jax import lax
from jax.experimental import pallas as pl
from jax.experimental.pallas import tpu as pltpu
from jax.sharding import PartitionSpec as P

CA = 8
H = 32
CHANNELS = 10
ROWS = CA + 6
LINES = ROWS * H
SEND = 4 * H

density_base = 0.5

WIDE = (0, 1, 2, 3, 4, 7, 8)
ORDER = (0, 1, 2, 3, 4, 7, 8, 5, 6, 9)
EARLY, FIRST = 2, 5

MESH = pl.DeviceIdType.MESH


def split(value):
    high = value.astype(jnp.bfloat16)
    low = (value - high.astype(jnp.float32)).astype(jnp.bfloat16)
    return high, low


def kernel(
    n_az, n_rad, count_ref, dest_in, mass_ref, flux_ref,
    smoothed_ref, force_ref, strain_ref,
    dest_ref, vin, high, low, weights, part, from_left, from_right,
    strip, strip_left, strip_right, edge_out, edge_left, edge_right,
    load_sem, send_sem, recv_sem, band_send, band_recv,
):
    sector = lax.axis_index("az")
    band = lax.axis_index("rad")
    slots = vin.shape[1]
    width = vin.shape[2]
    total_rows = CA * n_az
    right, left = lax.rem(sector + 1, n_az), lax.rem(sector + n_az - 1, n_az)
    outer, inner = band + 1, band - 1
    has_outer, has_inner = band < n_rad - 1, band > 0

    load_dest = pltpu.make_async_copy(dest_in, dest_ref, load_sem.at[CHANNELS])
    load_dest.start()
    loads = {}
    for c in ORDER:
        source = mass_ref if c == 0 else flux_ref.at[c - 1]
        loads[c] = pltpu.make_async_copy(source, vin.at[c], load_sem.at[c])
        loads[c].start()

    barrier = pltpu.get_barrier_semaphore()
    for neighbour in (left, right):
        pl.semaphore_signal(barrier, inc=1, device_id={"az": neighbour}, device_id_type=MESH)

    @pl.when(has_outer)
    def _():
        pl.semaphore_signal(barrier, inc=1, device_id={"rad": outer}, device_id_type=MESH)

    @pl.when(has_inner)
    def _():
        pl.semaphore_signal(barrier, inc=1, device_id={"rad": inner}, device_id_type=MESH)

    load_dest.wait()
    dest = dest_ref[...]
    live = lax.broadcasted_iota(jnp.int32, (1, slots), 1) < count_ref[0, 0]
    height = dest & (H - 1)
    offset = (dest >> 5) - sector * CA + 2
    offset = jnp.where(offset < 0, offset + total_rows, offset)
    offset = jnp.where(offset >= total_rows, offset - total_rows, offset)
    apart = jnp.abs(lax.broadcasted_iota(jnp.int32, (H, slots), 0) - height)
    by_height = jnp.where(apart == 0, 0.5, jnp.where(apart == 1, 0.25, 0.0))
    for i in range(ROWS):
        apart = jnp.abs(i - 1 - offset)
        by_row = jnp.where(apart == 0, 0.5, jnp.where(apart == 1, 0.25, 0.0))
        by_row = jnp.where(live, by_row, 0.0)
        weights[i * H : (i + 1) * H, :] = (by_height * by_row).astype(jnp.bfloat16)

    def unpack(c):
        loads[c].wait()
        top, rest = split(vin[c])
        high[:, c * width : (c + 1) * width] = top
        low[:, c * width : (c + 1) * width] = rest

    def dot(a, b):
        return jnp.dot(a, b, preferred_element_type=jnp.float32)

    def deposited(top, rest):
        both = dot(weights[...], jnp.concatenate([top, rest], axis=1))
        return both[:, :128] + both[:, 128:]

    sends = {}

    def send(name, source_right, target_left, source_left, target_right):
        pair = []
        for way, (source, target, device) in enumerate(
            ((source_right, target_left, right), (source_left, target_right, left))
        ):
            copy = pltpu.make_async_remote_copy(
                src_ref=source, dst_ref=target,
                send_sem=send_sem.at[way, name], recv_sem=recv_sem.at[way, name],
                device_id={"az": device}, device_id_type=MESH,
            )
            copy.start()
            pair.append(copy)
        sends[name] = pair

    def deposit(c):
        columns = slice(c * width, (c + 1) * width)
        part[c] = deposited(high[:, columns], low[:, columns])

    def send_channel(c):
        wide = c in WIDE
        size = SEND if wide else SEND - H
        skip = 0 if wide else H
        send(
            c,
            part.at[c, pl.ds(LINES - size, size)], from_left.at[c, pl.ds(skip, size)],
            part.at[c, pl.ds(0, size)], from_right.at[c, pl.ds(0, size)],
        )

    for c in ORDER[:EARLY]:
        unpack(c)
        deposit(c)
        if c == ORDER[0]:
            pl.semaphore_wait(
                barrier, 2 + has_outer.astype(jnp.int32) + has_inner.astype(jnp.int32)
            )
        send_channel(c)
    for c in ORDER[EARLY:]:
        unpack(c)

    depth = lax.broadcasted_iota(jnp.int32, (width, 128), 0)
    lane = lax.broadcasted_iota(jnp.int32, (width, 128), 1)
    place = lane // 20
    odd = lane % 2 == 1
    mirror = jnp.where(place == 1, jnp.where(odd, width - 2, 1), jnp.where(odd, width - 1, 0))
    mirror = jnp.where(place == 2, width - 1 - mirror, mirror)
    hit = (mirror == depth) & (place < 3)
    channel = (lane % 20) // 2
    select = jnp.concatenate(
        [jnp.where(hit & (channel == c), 1.0, 0.0).astype(jnp.bfloat16) for c in range(CHANNELS)],
        axis=0,
    )

    strip[...] = deposited(
        dot(high[...], select).astype(jnp.bfloat16), dot(low[...], select).astype(jnp.bfloat16)
    )
    to_outer = pltpu.make_async_remote_copy(
        src_ref=strip, dst_ref=strip_left, send_sem=band_send.at[0], recv_sem=band_recv.at[0],
        device_id={"rad": outer}, device_id_type=MESH,
    )
    to_inner = pltpu.make_async_remote_copy(
        src_ref=strip, dst_ref=strip_right, send_sem=band_send.at[1], recv_sem=band_recv.at[1],
        device_id={"rad": inner}, device_id_type=MESH,
    )

    @pl.when(has_outer)
    def _():
        to_outer.start()

    @pl.when(has_inner)
    def _():
        to_inner.start()

    for c in ORDER[EARLY:FIRST]:
        deposit(c)
        send_channel(c)
    for c in ORDER[FIRST:]:
        deposit(c)

    @pl.when(has_inner)
    def _():
        to_outer.wait_recv()

    @pl.when(jnp.logical_not(has_inner))
    def _():
        strip_left[...] = jnp.zeros_like(strip_left)

    @pl.when(has_outer)
    def _():
        to_inner.wait_recv()

    @pl.when(jnp.logical_not(has_outer))
    def _():
        strip_right[...] = jnp.zeros_like(strip_right)

    lane = lax.broadcasted_iota(jnp.int32, (LINES, 128), 1)
    beside = jnp.where(lane % 2 == 0, strip_right[...], strip_left[...])
    edges = jnp.where(lane < 40, beside, strip[...])
    edge_out[0] = jnp.transpose(edges[LINES - SEND :])[:64]
    edge_out[1] = jnp.transpose(edges[:SEND])[:64]
    send(CHANNELS, edge_out.at[0], edge_left, edge_out.at[1], edge_right)

    for c in ORDER[FIRST:]:
        send_channel(c)

    def arrived(name):
        for copy in sends[name]:
            copy.wait_recv()

    arrived(CHANNELS)
    nothing = jnp.zeros((64, 128), jnp.float32)
    edges = jnp.concatenate(
        [
            edges[2 * H : 6 * H] + jnp.transpose(jnp.concatenate([edge_left[...], nothing], axis=0)),
            edges[6 * H : 8 * H],
            edges[8 * H : 12 * H] + jnp.transpose(jnp.concatenate([edge_right[...], nothing], axis=0)),
        ],
        axis=0,
    )
    lines = (CA + 2) * H
    lane = lax.broadcasted_iota(jnp.int32, (1, 128), 1)
    inside = jnp.where(lane % 2 == 0, has_outer.astype(jnp.float32), has_inner.astype(jnp.float32))
    edge_smoothed = 0.5 * edges + 0.25 * (pltpu.roll(edges, 108, 1) + pltpu.roll(edges, 88, 1))
    edge_smoothed = edge_smoothed * inside
    edge_combined = edge_smoothed[H : H + CA * H]
    density = 1.0 / (edge_combined + density_base)
    for c in (1, 2, 3):
        own = (lane == 2 * c) | (lane == 2 * c + 1)
        edge_combined = edge_combined * jnp.where(own, pltpu.roll(density, 2 * c, 1), 1.0)

    def beside_in_band(value, edge, c):
        edge = pltpu.roll(edge, 127 - 2 * c, 1)
        return (
            jnp.where(lane == 0, edge, pltpu.roll(value, 1, 1)),
            jnp.where(lane == 127, edge, pltpu.roll(value, 127, 1)),
        )

    radius = (width * n_rad + band * width + lane).astype(jnp.float32) + 0.5
    scale_az = 0.5 / (radius * (2.0 * math.pi / total_rows))
    recip = 1.0 / radius
    cell = lax.broadcasted_iota(jnp.int32, (CA * H, 1), 0) & (H - 1)

    def smooth(c):
        arrived(c)
        if c in WIDE:
            total = jnp.concatenate(
                [
                    part[c, 2 * H : 6 * H] + from_left[c],
                    part[c, 6 * H : 8 * H],
                    part[c, 8 * H : 12 * H] + from_right[c],
                ],
                axis=0,
            )
            edge = edges
        else:
            total = jnp.concatenate(
                [
                    part[c, 3 * H : 6 * H] + from_left[c, H:],
                    part[c, 6 * H : 8 * H],
                    part[c, 8 * H : 11 * H] + from_right[c, : 3 * H],
                ],
                axis=0,
            )
            edge = edges[H : H + CA * H]
        before, after = beside_in_band(total, edge, c)
        result = 0.5 * total + 0.25 * (before + after)
        smoothed_ref[c] = result[H : H + CA * H] if c in WIDE else result
        return result

    def grad_az(value):
        return (value[2 * H :] - value[: CA * H]) * scale_az

    def center(value):
        return value[H : H + CA * H]

    def grad_rad(value, c):
        before, after = beside_in_band(value, edge_combined, c)
        return (after - before) * 0.5

    def grad_height(value):
        below = jnp.where(cell == 0, 0.0, pltpu.roll(value, 1, 0))
        above = jnp.where(cell == H - 1, 0.0, pltpu.roll(value, CA * H - 1, 0))
        return (above - below) * 0.5

    density = 1.0 / (smooth(0) + density_base)
    value = smooth(1) * density
    middle = center(value)
    strain_ref[0] = grad_az(value)
    strain_ref[3] = grad_height(middle)
    strain_ref[4] = grad_rad(middle, 1) - middle * recip
    value = smooth(2) * density
    middle = center(value)
    strain_ref[1] = grad_height(middle)
    strain_ref[3] = 0.5 * (strain_ref[3] + grad_az(value))
    strain_ref[5] = grad_rad(middle, 2)
    value = smooth(3) * density
    middle = center(value)
    strain_ref[0] += middle * recip
    strain_ref[2] = grad_rad(middle, 3)
    strain_ref[4] = 0.5 * (strain_ref[4] + grad_az(value))
    strain_ref[5] = 0.5 * (strain_ref[5] + grad_height(middle))
    value = smooth(4)
    force_ref[0] = grad_az(value)
    force_ref[2] = -center(value) * recip
    value = smooth(7)
    force_ref[0] += grad_height(center(value))
    force_ref[1] = grad_az(value)
    value = smooth(8)
    middle = center(value)
    force_ref[0] += grad_rad(middle, 8) + 2.0 * middle * recip
    force_ref[2] += grad_az(value)
    force_ref[1] += grad_height(smooth(5))
    middle = smooth(6)
    force_ref[2] += grad_rad(middle, 6) + middle * recip
    middle = smooth(9)
    force_ref[1] += grad_rad(middle, 9)
    force_ref[2] += grad_height(middle)

    for pair in sends.values():
        for copy in pair:
            copy.wait_send()

    @pl.when(has_outer)
    def _():
        to_outer.wait_send()

    @pl.when(has_inner)
    def _():
        to_inner.wait_send()


def store(smoothed, force, strain, smoothed_out, force_out, strain_out, sem):
    half = CHANNELS // 2
    copies = [
        pltpu.make_async_copy(source, target, sem.at[i])
        for i, (source, target) in enumerate(
            (
                (smoothed.at[pl.ds(0, half)], smoothed_out.at[pl.ds(0, half)]),
                (smoothed.at[pl.ds(half, half)], smoothed_out.at[pl.ds(half, half)]),
                (strain, strain_out),
                (force, force_out),
            )
        )
    ]
    for copy in copies:
        copy.start()
    for copy in copies:
        copy.wait()


def local(block_mass, block_flux, block_dest, block_count):
    n_az = lax.axis_size("az")
    n_rad = lax.axis_size("rad")
    slots, width = block_mass.shape[2:]
    cells = CA * H
    f32 = jnp.float32
    outs = pl.pallas_call(
        functools.partial(kernel, n_az, n_rad),
        out_shape=[pltpu.VMEM((k, cells, width), f32) for k in (CHANNELS, 3, 6)],
        in_specs=[
            pl.BlockSpec(memory_space=pltpu.SMEM),
            pl.BlockSpec(memory_space=pl.ANY),
            pl.BlockSpec(memory_space=pl.ANY),
            pl.BlockSpec(memory_space=pl.ANY),
        ],
        out_specs=[pl.BlockSpec(memory_space=pltpu.VMEM)] * 3,
        scratch_shapes=[
            pltpu.VMEM((1, slots), jnp.int32),
            pltpu.VMEM((CHANNELS, slots, width), f32),
            pltpu.VMEM((slots, CHANNELS * width), jnp.bfloat16),
            pltpu.VMEM((slots, CHANNELS * width), jnp.bfloat16),
            pltpu.VMEM((LINES, slots), jnp.bfloat16),
            pltpu.VMEM((CHANNELS, LINES, width), f32),
            pltpu.VMEM((CHANNELS, SEND, width), f32),
            pltpu.VMEM((CHANNELS, SEND, width), f32),
            pltpu.VMEM((LINES, 128), f32),
            pltpu.VMEM((LINES, 128), f32),
            pltpu.VMEM((LINES, 128), f32),
            pltpu.VMEM((2, 64, SEND), f32),
            pltpu.VMEM((64, SEND), f32),
            pltpu.VMEM((64, SEND), f32),
            pltpu.SemaphoreType.DMA((CHANNELS + 1,)),
            pltpu.SemaphoreType.DMA((2, CHANNELS + 1)),
            pltpu.SemaphoreType.DMA((2, CHANNELS + 1)),
            pltpu.SemaphoreType.DMA((2,)),
            pltpu.SemaphoreType.DMA((2,)),
        ],
        compiler_params=pltpu.CompilerParams(
            collective_id=0, has_side_effects=True, vmem_limit_bytes=56 * 1024 * 1024
        ),
    )(
        block_count,
        block_dest.reshape(1, slots),
        block_mass.reshape(slots, width),
        jnp.transpose(block_flux.reshape(slots, 9, width), (1, 0, 2)),
    )
    outs = pl.pallas_call(
        store,
        out_shape=[jax.ShapeDtypeStruct((k, cells, width), f32) for k in (CHANNELS, 3, 6)],
        in_specs=[pl.BlockSpec(memory_space=pltpu.VMEM)] * 3,
        out_specs=[pl.BlockSpec(memory_space=pltpu.HBM)] * 3,
        scratch_shapes=[pltpu.SemaphoreType.DMA((4,))],
        compiler_params=pltpu.CompilerParams(vmem_limit_bytes=8 * 1024 * 1024),
    )(*outs)
    return tuple(out.reshape(out.shape[0], CA, H, width) for out in outs)


def solution(mesh):
    return jax.shard_map(
        local,
        mesh=mesh,
        in_specs=(
            P("az", "rad", None, None),
            P("az", "rad", None, None, None),
            P("az", "rad", None),
            P("az", "rad"),
        ),
        out_specs=(
            P(None, "az", None, "rad"),
            P(None, "az", None, "rad"),
            P(None, "az", None, "rad"),
        ),
        check_vma=False,
    )
```

```python
import functools
import math

import jax
import jax.numpy as jnp
from jax import lax
from jax.experimental import pallas as pl
from jax.experimental.pallas import tpu as pltpu
from jax.sharding import PartitionSpec as P

CA = 8
H = 32
CHANNELS = 10
ROWS = CA + 6
LINES = ROWS * H
SEND = 4 * H
EDGES = 4 * CHANNELS

density_base = 0.5

WIDE = (0, 1, 2, 3, 4, 7, 8)
RADIAL = (0, 1, 2, 3, 6, 8, 9)
ORDER = (0, 1, 2, 3, 4, 7, 8, 5, 6, 9)
EARLY, FIRST = 2, 5

MESH = pl.DeviceIdType.MESH


def split(value):
    high = value.astype(jnp.bfloat16)
    low = (value - high.astype(jnp.float32)).astype(jnp.bfloat16)
    return high, low


def kernel(
    n_az, n_rad, count_ref, dest_in, mass_ref, flux_ref,
    smoothed_ref, force_ref, strain_ref,
    dest_ref, vin, high, low, weights, part, from_left, from_right,
    strip, strip_left, strip_right, edge_out, edge_left, edge_right,
    load_sem, send_sem, recv_sem, band_send, band_recv,
):
    sector = lax.axis_index("az")
    band = lax.axis_index("rad")
    slots = vin.shape[1]
    width = vin.shape[2]
    total_rows = CA * n_az
    right, left = lax.rem(sector + 1, n_az), lax.rem(sector + n_az - 1, n_az)
    outer, inner = band + 1, band - 1
    has_outer, has_inner = band < n_rad - 1, band > 0

    load_dest = pltpu.make_async_copy(dest_in, dest_ref, load_sem.at[CHANNELS])
    load_dest.start()
    loads = {}
    for c in ORDER:
        source = mass_ref if c == 0 else flux_ref.at[c - 1]
        loads[c] = pltpu.make_async_copy(source, vin.at[c], load_sem.at[c])
        loads[c].start()

    barrier = pltpu.get_barrier_semaphore()
    for neighbour in (left, right):
        pl.semaphore_signal(barrier, inc=1, device_id={"az": neighbour}, device_id_type=MESH)

    @pl.when(has_outer)
    def _():
        pl.semaphore_signal(barrier, inc=1, device_id={"rad": outer}, device_id_type=MESH)

    @pl.when(has_inner)
    def _():
        pl.semaphore_signal(barrier, inc=1, device_id={"rad": inner}, device_id_type=MESH)

    load_dest.wait()
    dest = dest_ref[...]
    live = lax.broadcasted_iota(jnp.int32, (1, slots), 1) < count_ref[0, 0]
    height = dest & (H - 1)
    offset = (dest >> 5) - sector * CA + 2
    offset = jnp.where(offset < 0, offset + total_rows, offset)
    offset = jnp.where(offset >= total_rows, offset - total_rows, offset)
    apart = jnp.abs(lax.broadcasted_iota(jnp.int32, (H, slots), 0) - height)
    by_height = jnp.where(apart == 0, 0.5, jnp.where(apart == 1, 0.25, 0.0))
    for i in range(ROWS):
        apart = jnp.abs(i - 1 - offset)
        by_row = jnp.where(apart == 0, 0.5, jnp.where(apart == 1, 0.25, 0.0))
        by_row = jnp.where(live, by_row, 0.0)
        weights[i * H : (i + 1) * H, :] = (by_height * by_row).astype(jnp.bfloat16)

    def unpack(c):
        loads[c].wait()
        top, rest = split(vin[c])
        high[:, c * width : (c + 1) * width] = top
        low[:, c * width : (c + 1) * width] = rest

    def dot(a, b):
        return jnp.dot(a, b, preferred_element_type=jnp.float32)

    def deposited(top, rest):
        both = dot(weights[...], jnp.concatenate([top, rest], axis=1))
        return both[:, :128] + both[:, 128:]

    sends = {}

    def send(name, source_right, target_left, source_left, target_right):
        pair = []
        for way, (source, target, device) in enumerate(
            ((source_right, target_left, right), (source_left, target_right, left))
        ):
            copy = pltpu.make_async_remote_copy(
                src_ref=source, dst_ref=target,
                send_sem=send_sem.at[way, name], recv_sem=recv_sem.at[way, name],
                device_id={"az": device}, device_id_type=MESH,
            )
            copy.start()
            pair.append(copy)
        sends[name] = pair

    def deposit(c):
        columns = slice(c * width, (c + 1) * width)
        part[c] = deposited(high[:, columns], low[:, columns])

    def send_channel(c):
        wide = c in WIDE
        size = SEND if wide else SEND - H
        skip = 0 if wide else H
        send(
            c,
            part.at[c, pl.ds(LINES - size, size)], from_left.at[c, pl.ds(skip, size)],
            part.at[c, pl.ds(0, size)], from_right.at[c, pl.ds(0, size)],
        )

    for c in ORDER[:EARLY]:
        unpack(c)
        deposit(c)
        if c == ORDER[0]:
            pl.semaphore_wait(
                barrier, 2 + has_outer.astype(jnp.int32) + has_inner.astype(jnp.int32)
            )
        send_channel(c)
    for c in ORDER[EARLY:]:
        unpack(c)

    depth = lax.broadcasted_iota(jnp.int32, (width, 128), 0)
    lane = lax.broadcasted_iota(jnp.int32, (width, 128), 1)
    place = lane // 20
    odd = lane % 2 == 1
    mirror = jnp.where(place == 1, jnp.where(odd, width - 2, 1), jnp.where(odd, width - 1, 0))
    hit = (mirror == depth) & (place < 2)
    channel = (lane % 20) // 2
    select = jnp.concatenate(
        [jnp.where(hit & (channel == c), 1.0, 0.0).astype(jnp.bfloat16) for c in range(CHANNELS)],
        axis=0,
    )

    strip[...] = deposited(
        dot(high[...], select).astype(jnp.bfloat16), dot(low[...], select).astype(jnp.bfloat16)
    )
    to_outer = pltpu.make_async_remote_copy(
        src_ref=strip, dst_ref=strip_left, send_sem=band_send.at[0], recv_sem=band_recv.at[0],
        device_id={"rad": outer}, device_id_type=MESH,
    )
    to_inner = pltpu.make_async_remote_copy(
        src_ref=strip, dst_ref=strip_right, send_sem=band_send.at[1], recv_sem=band_recv.at[1],
        device_id={"rad": inner}, device_id_type=MESH,
    )

    @pl.when(has_outer)
    def _():
        to_outer.start()

    @pl.when(has_inner)
    def _():
        to_inner.start()

    for c in ORDER[EARLY:FIRST]:
        deposit(c)
        send_channel(c)
    for c in ORDER[FIRST:]:
        deposit(c)

    @pl.when(has_inner)
    def _():
        to_outer.wait_recv()

    @pl.when(jnp.logical_not(has_inner))
    def _():
        strip_left[...] = jnp.zeros_like(strip_left)

    @pl.when(has_outer)
    def _():
        to_inner.wait_recv()

    @pl.when(jnp.logical_not(has_outer))
    def _():
        strip_right[...] = jnp.zeros_like(strip_right)

    lane = lax.broadcasted_iota(jnp.int32, (LINES, 128), 1)
    edges = jnp.where(lane % 2 == 0, strip_right[...], strip_left[...])
    edge_out[0] = jnp.transpose(edges[LINES - SEND :])[:EDGES]
    edge_out[1] = jnp.transpose(edges[:SEND])[:EDGES]
    send(CHANNELS, edge_out.at[0], edge_left, edge_out.at[1], edge_right)

    for c in ORDER[FIRST:]:
        send_channel(c)

    def arrived(name):
        for copy in sends[name]:
            copy.wait_recv()

    arrived(CHANNELS)
    nothing = jnp.zeros((128 - EDGES, 128), jnp.float32)
    edges = jnp.concatenate(
        [
            edges[2 * H : 6 * H] + jnp.transpose(jnp.concatenate([edge_left[...], nothing], axis=0)),
            edges[6 * H : 8 * H],
            edges[8 * H : 12 * H] + jnp.transpose(jnp.concatenate([edge_right[...], nothing], axis=0)),
        ],
        axis=0,
    )
    lane = lax.broadcasted_iota(jnp.int32, (1, 128), 1)
    inside = jnp.where(lane == 0, has_inner.astype(jnp.float32), has_outer.astype(jnp.float32))

    def beside_in_band(value, edge):
        return (
            jnp.where(lane == 0, edge, pltpu.roll(value, 1, 1)),
            jnp.where(lane == 127, edge, pltpu.roll(value, 127, 1)),
        )

    radius = (width * n_rad + band * width + lane).astype(jnp.float32) + 0.5
    scale_az = 0.5 / (radius * (2.0 * math.pi / total_rows))
    recip = 1.0 / radius
    cell = lax.broadcasted_iota(jnp.int32, (CA * H, 1), 0) & (H - 1)

    def smooth(c):
        arrived(c)
        if c in WIDE:
            total = jnp.concatenate(
                [
                    part[c, 2 * H : 6 * H] + from_left[c],
                    part[c, 6 * H : 8 * H],
                    part[c, 8 * H : 12 * H] + from_right[c],
                ],
                axis=0,
            )
            edge = edges
        else:
            total = jnp.concatenate(
                [
                    part[c, 3 * H : 6 * H] + from_left[c, H:],
                    part[c, 6 * H : 8 * H],
                    part[c, 8 * H : 11 * H] + from_right[c, : 3 * H],
                ],
                axis=0,
            )
            edge = edges[H : H + CA * H]
        near = pltpu.roll(edge, 127 - 2 * c, 1)
        before, after = beside_in_band(total, near)
        result = 0.5 * total + 0.25 * (before + after)
        smoothed_ref[c] = center(result) if c in WIDE else result
        if c not in RADIAL:
            return result
        if c in WIDE:
            edge, near, total = center(edge), center(near), center(total)
        far = pltpu.roll(edge, 107 - 2 * c, 1)
        return result, (0.5 * near + 0.25 * (far + total)) * inside

    def grad_az(value):
        return (value[2 * H :] - value[: CA * H]) * scale_az

    def center(value):
        return value[H : H + CA * H]

    def grad_rad(value, edge):
        before, after = beside_in_band(value, edge)
        return (after - before) * 0.5

    def grad_height(value):
        below = jnp.where(cell == 0, 0.0, pltpu.roll(value, 1, 0))
        above = jnp.where(cell == H - 1, 0.0, pltpu.roll(value, CA * H - 1, 0))
        return (above - below) * 0.5

    value, edge = smooth(0)
    density, edge_density = 1.0 / (value + density_base), 1.0 / (edge + density_base)
    value, edge = smooth(1)
    value, edge = value * density, edge * edge_density
    middle = center(value)
    strain_ref[0] = grad_az(value)
    strain_ref[3] = grad_height(middle)
    strain_ref[4] = grad_rad(middle, edge) - middle * recip
    value, edge = smooth(2)
    value, edge = value * density, edge * edge_density
    middle = center(value)
    strain_ref[1] = grad_height(middle)
    strain_ref[3] = 0.5 * (strain_ref[3] + grad_az(value))
    strain_ref[5] = grad_rad(middle, edge)
    value, edge = smooth(3)
    value, edge = value * density, edge * edge_density
    middle = center(value)
    strain_ref[0] += middle * recip
    strain_ref[2] = grad_rad(middle, edge)
    strain_ref[4] = 0.5 * (strain_ref[4] + grad_az(value))
    strain_ref[5] = 0.5 * (strain_ref[5] + grad_height(middle))
    value = smooth(4)
    force_ref[0] = grad_az(value)
    force_ref[2] = -center(value) * recip
    value = smooth(7)
    force_ref[0] += grad_height(center(value))
    force_ref[1] = grad_az(value)
    value, edge = smooth(8)
    middle = center(value)
    force_ref[0] += grad_rad(middle, edge) + 2.0 * middle * recip
    force_ref[2] += grad_az(value)
    force_ref[1] += grad_height(smooth(5))
    middle, edge = smooth(6)
    force_ref[2] += grad_rad(middle, edge) + middle * recip
    middle, edge = smooth(9)
    force_ref[1] += grad_rad(middle, edge)
    force_ref[2] += grad_height(middle)

    for pair in sends.values():
        for copy in pair:
            copy.wait_send()

    @pl.when(has_outer)
    def _():
        to_outer.wait_send()

    @pl.when(has_inner)
    def _():
        to_inner.wait_send()


def store(smoothed, force, strain, smoothed_out, force_out, strain_out, sem):
    copies = []
    for source, target in ((smoothed, smoothed_out), (strain, strain_out), (force, force_out)):
        for k in range(source.shape[0]):
            copy = pltpu.make_async_copy(source.at[k], target.at[k], sem.at[len(copies)])
            copy.start()
            copies.append(copy)
    for copy in copies:
        copy.wait()


def local(block_mass, block_flux, block_dest, block_count):
    n_az = lax.axis_size("az")
    n_rad = lax.axis_size("rad")
    slots, width = block_mass.shape[2:]
    cells = CA * H
    f32 = jnp.float32
    outs = pl.pallas_call(
        functools.partial(kernel, n_az, n_rad),
        out_shape=[pltpu.VMEM((k, cells, width), f32) for k in (CHANNELS, 3, 6)],
        in_specs=[
            pl.BlockSpec(memory_space=pltpu.SMEM),
            pl.BlockSpec(memory_space=pl.ANY),
            pl.BlockSpec(memory_space=pl.ANY),
            pl.BlockSpec(memory_space=pl.ANY),
        ],
        out_specs=[pl.BlockSpec(memory_space=pltpu.VMEM)] * 3,
        scratch_shapes=[
            pltpu.VMEM((1, slots), jnp.int32),
            pltpu.VMEM((CHANNELS, slots, width), f32),
            pltpu.VMEM((slots, CHANNELS * width), jnp.bfloat16),
            pltpu.VMEM((slots, CHANNELS * width), jnp.bfloat16),
            pltpu.VMEM((LINES, slots), jnp.bfloat16),
            pltpu.VMEM((CHANNELS, LINES, width), f32),
            pltpu.VMEM((CHANNELS, SEND, width), f32),
            pltpu.VMEM((CHANNELS, SEND, width), f32),
            pltpu.VMEM((LINES, 128), f32),
            pltpu.VMEM((LINES, 128), f32),
            pltpu.VMEM((LINES, 128), f32),
            pltpu.VMEM((2, EDGES, SEND), f32),
            pltpu.VMEM((EDGES, SEND), f32),
            pltpu.VMEM((EDGES, SEND), f32),
            pltpu.SemaphoreType.DMA((CHANNELS + 1,)),
            pltpu.SemaphoreType.DMA((2, CHANNELS + 1)),
            pltpu.SemaphoreType.DMA((2, CHANNELS + 1)),
            pltpu.SemaphoreType.DMA((2,)),
            pltpu.SemaphoreType.DMA((2,)),
        ],
        compiler_params=pltpu.CompilerParams(
            collective_id=0, has_side_effects=True, vmem_limit_bytes=56 * 1024 * 1024
        ),
    )(
        block_count,
        block_dest.reshape(1, slots),
        block_mass.reshape(slots, width),
        jnp.transpose(block_flux.reshape(slots, 9, width), (1, 0, 2)),
    )
    outs = pl.pallas_call(
        store,
        out_shape=[jax.ShapeDtypeStruct((k, cells, width), f32) for k in (CHANNELS, 3, 6)],
        in_specs=[pl.BlockSpec(memory_space=pltpu.VMEM)] * 3,
        out_specs=[pl.BlockSpec(memory_space=pltpu.HBM)] * 3,
        scratch_shapes=[pltpu.SemaphoreType.DMA((CHANNELS + 9,))],
        compiler_params=pltpu.CompilerParams(vmem_limit_bytes=8 * 1024 * 1024),
    )(*outs)
    return tuple(out.reshape(out.shape[0], CA, H, width) for out in outs)


def solution(mesh):
    return jax.shard_map(
        local,
        mesh=mesh,
        in_specs=(
            P("az", "rad", None, None),
            P("az", "rad", None, None, None),
            P("az", "rad", None),
            P("az", "rad"),
        ),
        out_specs=(
            P(None, "az", None, "rad"),
            P(None, "az", None, "rad"),
            P(None, "az", None, "rad"),
        ),
        check_vma=False,
    )
```

```python
import functools
import math

import jax
import jax.numpy as jnp
from jax import lax
from jax.experimental import pallas as pl
from jax.experimental.pallas import tpu as pltpu
from jax.sharding import PartitionSpec as P

CA = 8
H = 32
CHANNELS = 10
ROWS = CA + 6
LINES = ROWS * H
SEND = 4 * H
EDGES = 4 * CHANNELS

density_base = 0.5

WIDE = (0, 1, 2, 3, 4, 7, 8)
RADIAL = (0, 1, 2, 3, 6, 8, 9)
ORDER = (0, 1, 2, 3, 4, 7, 8, 5, 6, 9)
EARLY, FIRST = 2, 8

MESH = pl.DeviceIdType.MESH


def split(value):
    high = value.astype(jnp.bfloat16)
    low = (value - high.astype(jnp.float32)).astype(jnp.bfloat16)
    return high, low


def kernel(
    n_az, n_rad, count_ref, dest_in, mass_ref, flux_ref,
    smoothed_ref, force_ref, strain_ref,
    dest_ref, vin, high, low, weights, part, from_left, from_right,
    strip, strip_left, strip_right, edge_out, edge_left, edge_right,
    load_sem, send_sem, recv_sem, band_send, band_recv,
):
    sector = lax.axis_index("az")
    band = lax.axis_index("rad")
    slots = vin.shape[1]
    width = vin.shape[2]
    total_rows = CA * n_az
    right, left = lax.rem(sector + 1, n_az), lax.rem(sector + n_az - 1, n_az)
    outer, inner = band + 1, band - 1
    has_outer, has_inner = band < n_rad - 1, band > 0

    load_dest = pltpu.make_async_copy(dest_in, dest_ref, load_sem.at[CHANNELS])
    load_dest.start()
    loads = {}
    for c in ORDER:
        source = mass_ref if c == 0 else flux_ref.at[c - 1]
        loads[c] = pltpu.make_async_copy(source, vin.at[c], load_sem.at[c])
        loads[c].start()

    barrier = pltpu.get_barrier_semaphore()
    for neighbour in (left, right):
        pl.semaphore_signal(barrier, inc=1, device_id={"az": neighbour}, device_id_type=MESH)

    @pl.when(has_outer)
    def _():
        pl.semaphore_signal(barrier, inc=1, device_id={"rad": outer}, device_id_type=MESH)

    @pl.when(has_inner)
    def _():
        pl.semaphore_signal(barrier, inc=1, device_id={"rad": inner}, device_id_type=MESH)

    load_dest.wait()
    dest = dest_ref[...]
    live = lax.broadcasted_iota(jnp.int32, (1, slots), 1) < count_ref[0, 0]
    height = dest & (H - 1)
    offset = (dest >> 5) - sector * CA + 2
    offset = jnp.where(offset < 0, offset + total_rows, offset)
    offset = jnp.where(offset >= total_rows, offset - total_rows, offset)
    apart = jnp.abs(lax.broadcasted_iota(jnp.int32, (H, slots), 0) - height)
    by_height = jnp.where(apart == 0, 0.5, jnp.where(apart == 1, 0.25, 0.0))
    for i in range(ROWS):
        apart = jnp.abs(i - 1 - offset)
        by_row = jnp.where(apart == 0, 0.5, jnp.where(apart == 1, 0.25, 0.0))
        by_row = jnp.where(live, by_row, 0.0)
        weights[i * H : (i + 1) * H, :] = (by_height * by_row).astype(jnp.bfloat16)

    def unpack(c):
        loads[c].wait()
        top, rest = split(vin[c])
        high[:, c * width : (c + 1) * width] = top
        low[:, c * width : (c + 1) * width] = rest

    def dot(a, b):
        return jnp.dot(a, b, preferred_element_type=jnp.float32)

    def deposited(top, rest):
        both = dot(weights[...], jnp.concatenate([top, rest], axis=1))
        return both[:, :128] + both[:, 128:]

    sends = {}

    def send(name, source_right, target_left, source_left, target_right):
        pair = []
        for way, (source, target, device) in enumerate(
            ((source_right, target_left, right), (source_left, target_right, left))
        ):
            copy = pltpu.make_async_remote_copy(
                src_ref=source, dst_ref=target,
                send_sem=send_sem.at[way, name], recv_sem=recv_sem.at[way, name],
                device_id={"az": device}, device_id_type=MESH,
            )
            copy.start()
            pair.append(copy)
        sends[name] = pair

    def deposit(c):
        columns = slice(c * width, (c + 1) * width)
        part[c] = deposited(high[:, columns], low[:, columns])

    def send_channel(c):
        wide = c in WIDE
        size = SEND if wide else SEND - H
        skip = 0 if wide else H
        send(
            c,
            part.at[c, pl.ds(LINES - size, size)], from_left.at[c, pl.ds(skip, size)],
            part.at[c, pl.ds(0, size)], from_right.at[c, pl.ds(0, size)],
        )

    for c in ORDER[:EARLY]:
        unpack(c)
        deposit(c)
        if c == ORDER[0]:
            pl.semaphore_wait(
                barrier, 2 + has_outer.astype(jnp.int32) + has_inner.astype(jnp.int32)
            )
        send_channel(c)
    for c in ORDER[EARLY:]:
        unpack(c)

    depth = lax.broadcasted_iota(jnp.int32, (width, 128), 0)
    lane = lax.broadcasted_iota(jnp.int32, (width, 128), 1)
    place = lane // 20
    odd = lane % 2 == 1
    mirror = jnp.where(place == 1, jnp.where(odd, width - 2, 1), jnp.where(odd, width - 1, 0))
    hit = (mirror == depth) & (place < 2)
    channel = (lane % 20) // 2
    select = jnp.concatenate(
        [jnp.where(hit & (channel == c), 1.0, 0.0).astype(jnp.bfloat16) for c in range(CHANNELS)],
        axis=0,
    )

    strip[...] = deposited(
        dot(high[...], select).astype(jnp.bfloat16), dot(low[...], select).astype(jnp.bfloat16)
    )
    to_outer = pltpu.make_async_remote_copy(
        src_ref=strip, dst_ref=strip_left, send_sem=band_send.at[0], recv_sem=band_recv.at[0],
        device_id={"rad": outer}, device_id_type=MESH,
    )
    to_inner = pltpu.make_async_remote_copy(
        src_ref=strip, dst_ref=strip_right, send_sem=band_send.at[1], recv_sem=band_recv.at[1],
        device_id={"rad": inner}, device_id_type=MESH,
    )

    @pl.when(has_outer)
    def _():
        to_outer.start()

    @pl.when(has_inner)
    def _():
        to_inner.start()

    for c in ORDER[EARLY:FIRST]:
        deposit(c)
        send_channel(c)
    for c in ORDER[FIRST:]:
        deposit(c)

    @pl.when(has_inner)
    def _():
        to_outer.wait_recv()

    @pl.when(jnp.logical_not(has_inner))
    def _():
        strip_left[...] = jnp.zeros_like(strip_left)

    @pl.when(has_outer)
    def _():
        to_inner.wait_recv()

    @pl.when(jnp.logical_not(has_outer))
    def _():
        strip_right[...] = jnp.zeros_like(strip_right)

    lane = lax.broadcasted_iota(jnp.int32, (LINES, 128), 1)
    edges = jnp.where(lane % 2 == 0, strip_right[...], strip_left[...])
    edge_out[0] = jnp.transpose(edges[LINES - SEND :])[:EDGES]
    edge_out[1] = jnp.transpose(edges[:SEND])[:EDGES]
    send(CHANNELS, edge_out.at[0], edge_left, edge_out.at[1], edge_right)

    for c in ORDER[FIRST:]:
        send_channel(c)

    def arrived(name):
        for copy in sends[name]:
            copy.wait_recv()

    arrived(CHANNELS)
    nothing = jnp.zeros((128 - EDGES, 128), jnp.float32)
    edges = jnp.concatenate(
        [
            edges[2 * H : 6 * H] + jnp.transpose(jnp.concatenate([edge_left[...], nothing], axis=0)),
            edges[6 * H : 8 * H],
            edges[8 * H : 12 * H] + jnp.transpose(jnp.concatenate([edge_right[...], nothing], axis=0)),
        ],
        axis=0,
    )
    lane = lax.broadcasted_iota(jnp.int32, (1, 128), 1)
    inside = jnp.where(lane == 0, has_inner.astype(jnp.float32), has_outer.astype(jnp.float32))

    def beside_in_band(value, edge):
        return (
            jnp.where(lane == 0, edge, pltpu.roll(value, 1, 1)),
            jnp.where(lane == 127, edge, pltpu.roll(value, 127, 1)),
        )

    radius = (width * n_rad + band * width + lane).astype(jnp.float32) + 0.5
    scale_az = 0.5 / (radius * (2.0 * math.pi / total_rows))
    recip = 1.0 / radius
    cell = lax.broadcasted_iota(jnp.int32, (CA * H, 1), 0) & (H - 1)

    def smooth(c):
        arrived(c)
        if c in WIDE:
            total = jnp.concatenate(
                [
                    part[c, 2 * H : 6 * H] + from_left[c],
                    part[c, 6 * H : 8 * H],
                    part[c, 8 * H : 12 * H] + from_right[c],
                ],
                axis=0,
            )
            edge = edges
        else:
            total = jnp.concatenate(
                [
                    part[c, 3 * H : 6 * H] + from_left[c, H:],
                    part[c, 6 * H : 8 * H],
                    part[c, 8 * H : 11 * H] + from_right[c, : 3 * H],
                ],
                axis=0,
            )
            edge = edges[H : H + CA * H]
        near = pltpu.roll(edge, 127 - 2 * c, 1)
        before, after = beside_in_band(total, near)
        result = 0.5 * total + 0.25 * (before + after)
        smoothed_ref[c] = center(result) if c in WIDE else result
        if c not in RADIAL:
            return result
        if c in WIDE:
            edge, near, total = center(edge), center(near), center(total)
        far = pltpu.roll(edge, 107 - 2 * c, 1)
        return result, (0.5 * near + 0.25 * (far + total)) * inside

    def grad_az(value):
        return (value[2 * H :] - value[: CA * H]) * scale_az

    def center(value):
        return value[H : H + CA * H]

    def grad_rad(value, edge):
        before, after = beside_in_band(value, edge)
        return (after - before) * 0.5

    def grad_height(value):
        below = jnp.where(cell == 0, 0.0, pltpu.roll(value, 1, 0))
        above = jnp.where(cell == H - 1, 0.0, pltpu.roll(value, CA * H - 1, 0))
        return (above - below) * 0.5

    value, edge = smooth(0)
    density, edge_density = 1.0 / (value + density_base), 1.0 / (edge + density_base)
    value, edge = smooth(1)
    value, edge = value * density, edge * edge_density
    middle = center(value)
    strain_ref[0] = grad_az(value)
    strain_ref[3] = grad_height(middle)
    strain_ref[4] = grad_rad(middle, edge) - middle * recip
    value, edge = smooth(2)
    value, edge = value * density, edge * edge_density
    middle = center(value)
    strain_ref[1] = grad_height(middle)
    strain_ref[3] = 0.5 * (strain_ref[3] + grad_az(value))
    strain_ref[5] = grad_rad(middle, edge)
    value, edge = smooth(3)
    value, edge = value * density, edge * edge_density
    middle = center(value)
    strain_ref[0] += middle * recip
    strain_ref[2] = grad_rad(middle, edge)
    strain_ref[4] = 0.5 * (strain_ref[4] + grad_az(value))
    strain_ref[5] = 0.5 * (strain_ref[5] + grad_height(middle))
    value = smooth(4)
    force_ref[0] = grad_az(value)
    force_ref[2] = -center(value) * recip
    value = smooth(7)
    force_ref[0] += grad_height(center(value))
    force_ref[1] = grad_az(value)
    value, edge = smooth(8)
    middle = center(value)
    force_ref[0] += grad_rad(middle, edge) + 2.0 * middle * recip
    force_ref[2] += grad_az(value)
    force_ref[1] += grad_height(smooth(5))
    middle, edge = smooth(6)
    force_ref[2] += grad_rad(middle, edge) + middle * recip
    middle, edge = smooth(9)
    force_ref[1] += grad_rad(middle, edge)
    force_ref[2] += grad_height(middle)

    for pair in sends.values():
        for copy in pair:
            copy.wait_send()

    @pl.when(has_outer)
    def _():
        to_outer.wait_send()

    @pl.when(has_inner)
    def _():
        to_inner.wait_send()


def store(smoothed, force, strain, smoothed_out, force_out, strain_out, sem):
    half = CHANNELS // 2
    copies = [
        pltpu.make_async_copy(source, target, sem.at[i])
        for i, (source, target) in enumerate(
            (
                (smoothed.at[pl.ds(0, half)], smoothed_out.at[pl.ds(0, half)]),
                (smoothed.at[pl.ds(half, half)], smoothed_out.at[pl.ds(half, half)]),
                (strain, strain_out),
                (force, force_out),
            )
        )
    ]
    for copy in copies:
        copy.start()
    for copy in copies:
        copy.wait()


def local(block_mass, block_flux, block_dest, block_count):
    n_az = lax.axis_size("az")
    n_rad = lax.axis_size("rad")
    slots, width = block_mass.shape[2:]
    cells = CA * H
    f32 = jnp.float32
    outs = pl.pallas_call(
        functools.partial(kernel, n_az, n_rad),
        out_shape=[pltpu.VMEM((k, cells, width), f32) for k in (CHANNELS, 3, 6)],
        in_specs=[
            pl.BlockSpec(memory_space=pltpu.SMEM),
            pl.BlockSpec(memory_space=pl.ANY),
            pl.BlockSpec(memory_space=pl.ANY),
            pl.BlockSpec(memory_space=pl.ANY),
        ],
        out_specs=[pl.BlockSpec(memory_space=pltpu.VMEM)] * 3,
        scratch_shapes=[
            pltpu.VMEM((1, slots), jnp.int32),
            pltpu.VMEM((CHANNELS, slots, width), f32),
            pltpu.VMEM((slots, CHANNELS * width), jnp.bfloat16),
            pltpu.VMEM((slots, CHANNELS * width), jnp.bfloat16),
            pltpu.VMEM((LINES, slots), jnp.bfloat16),
            pltpu.VMEM((CHANNELS, LINES, width), f32),
            pltpu.VMEM((CHANNELS, SEND, width), f32),
            pltpu.VMEM((CHANNELS, SEND, width), f32),
            pltpu.VMEM((LINES, 128), f32),
            pltpu.VMEM((LINES, 128), f32),
            pltpu.VMEM((LINES, 128), f32),
            pltpu.VMEM((2, EDGES, SEND), f32),
            pltpu.VMEM((EDGES, SEND), f32),
            pltpu.VMEM((EDGES, SEND), f32),
            pltpu.SemaphoreType.DMA((CHANNELS + 1,)),
            pltpu.SemaphoreType.DMA((2, CHANNELS + 1)),
            pltpu.SemaphoreType.DMA((2, CHANNELS + 1)),
            pltpu.SemaphoreType.DMA((2,)),
            pltpu.SemaphoreType.DMA((2,)),
        ],
        compiler_params=pltpu.CompilerParams(
            collective_id=0, has_side_effects=True, vmem_limit_bytes=56 * 1024 * 1024
        ),
    )(
        block_count,
        block_dest.reshape(1, slots),
        block_mass.reshape(slots, width),
        jnp.transpose(block_flux.reshape(slots, 9, width), (1, 0, 2)),
    )
    outs = pl.pallas_call(
        store,
        out_shape=[jax.ShapeDtypeStruct((k, cells, width), f32) for k in (CHANNELS, 3, 6)],
        in_specs=[pl.BlockSpec(memory_space=pltpu.VMEM)] * 3,
        out_specs=[pl.BlockSpec(memory_space=pltpu.HBM)] * 3,
        scratch_shapes=[pltpu.SemaphoreType.DMA((4,))],
        compiler_params=pltpu.CompilerParams(vmem_limit_bytes=8 * 1024 * 1024),
    )(*outs)
    return tuple(out.reshape(out.shape[0], CA, H, width) for out in outs)


def solution(mesh):
    return jax.shard_map(
        local,
        mesh=mesh,
        in_specs=(
            P("az", "rad", None, None),
            P("az", "rad", None, None, None),
            P("az", "rad", None),
            P("az", "rad"),
        ),
        out_specs=(
            P(None, "az", None, "rad"),
            P(None, "az", None, "rad"),
            P(None, "az", None, "rad"),
        ),
        check_vma=False,
    )
```

```python
import functools
import math

import jax
import jax.numpy as jnp
from jax import lax
from jax.experimental import pallas as pl
from jax.experimental.pallas import tpu as pltpu
from jax.sharding import PartitionSpec as P

CA = 8
H = 32
CHANNELS = 10
ROWS = CA + 6
LINES = ROWS * H
SEND = 4 * H
EDGES = 4 * CHANNELS

density_base = 0.5

WIDE = (0, 1, 2, 3, 4, 7, 8)
RADIAL = (0, 1, 2, 3, 6, 8, 9)
ORDER = (0, 1, 2, 3, 4, 7, 8, 5, 6, 9)
EARLY, FIRST = 4, 8

MESH = pl.DeviceIdType.MESH


def split(value):
    high = value.astype(jnp.bfloat16)
    low = (value - high.astype(jnp.float32)).astype(jnp.bfloat16)
    return high, low


def kernel(
    n_az, n_rad, count_ref, dest_in, mass_ref, flux_ref,
    smoothed_ref, force_ref, strain_ref,
    dest_ref, vin, high, low, weights, part, from_left, from_right,
    strip, strip_left, strip_right, edge_out, edge_left, edge_right,
    load_sem, send_sem, recv_sem, band_send, band_recv,
):
    sector = lax.axis_index("az")
    band = lax.axis_index("rad")
    slots = vin.shape[1]
    width = vin.shape[2]
    total_rows = CA * n_az
    right, left = lax.rem(sector + 1, n_az), lax.rem(sector + n_az - 1, n_az)
    outer, inner = band + 1, band - 1
    has_outer, has_inner = band < n_rad - 1, band > 0

    load_dest = pltpu.make_async_copy(dest_in, dest_ref, load_sem.at[CHANNELS])
    load_dest.start()
    loads = {}
    for c in ORDER:
        source = mass_ref if c == 0 else flux_ref.at[c - 1]
        loads[c] = pltpu.make_async_copy(source, vin.at[c], load_sem.at[c])
        loads[c].start()

    barrier = pltpu.get_barrier_semaphore()
    for neighbour in (left, right):
        pl.semaphore_signal(barrier, inc=1, device_id={"az": neighbour}, device_id_type=MESH)

    @pl.when(has_outer)
    def _():
        pl.semaphore_signal(barrier, inc=1, device_id={"rad": outer}, device_id_type=MESH)

    @pl.when(has_inner)
    def _():
        pl.semaphore_signal(barrier, inc=1, device_id={"rad": inner}, device_id_type=MESH)

    load_dest.wait()
    dest = dest_ref[...]
    live = lax.broadcasted_iota(jnp.int32, (1, slots), 1) < count_ref[0, 0]
    height = dest & (H - 1)
    offset = (dest >> 5) - sector * CA + 2
    offset = jnp.where(offset < 0, offset + total_rows, offset)
    offset = jnp.where(offset >= total_rows, offset - total_rows, offset)
    apart = jnp.abs(lax.broadcasted_iota(jnp.int32, (H, slots), 0) - height)
    by_height = jnp.where(apart == 0, 0.5, jnp.where(apart == 1, 0.25, 0.0))
    for i in range(ROWS):
        apart = jnp.abs(i - 1 - offset)
        by_row = jnp.where(apart == 0, 0.5, jnp.where(apart == 1, 0.25, 0.0))
        by_row = jnp.where(live, by_row, 0.0)
        weights[i * H : (i + 1) * H, :] = (by_height * by_row).astype(jnp.bfloat16)

    def unpack(c):
        loads[c].wait()
        top, rest = split(vin[c])
        high[:, c * width : (c + 1) * width] = top
        low[:, c * width : (c + 1) * width] = rest

    def dot(a, b):
        return jnp.dot(a, b, preferred_element_type=jnp.float32)

    def deposited(top, rest):
        both = dot(weights[...], jnp.concatenate([top, rest], axis=1))
        return both[:, :128] + both[:, 128:]

    sends = {}

    def send(name, source_right, target_left, source_left, target_right):
        pair = []
        for way, (source, target, device) in enumerate(
            ((source_right, target_left, right), (source_left, target_right, left))
        ):
            copy = pltpu.make_async_remote_copy(
                src_ref=source, dst_ref=target,
                send_sem=send_sem.at[way, name], recv_sem=recv_sem.at[way, name],
                device_id={"az": device}, device_id_type=MESH,
            )
            copy.start()
            pair.append(copy)
        sends[name] = pair

    def deposit(c):
        columns = slice(c * width, (c + 1) * width)
        part[c] = deposited(high[:, columns], low[:, columns])

    def send_channel(c):
        wide = c in WIDE
        size = SEND if wide else SEND - H
        skip = 0 if wide else H
        send(
            c,
            part.at[c, pl.ds(LINES - size, size)], from_left.at[c, pl.ds(skip, size)],
            part.at[c, pl.ds(0, size)], from_right.at[c, pl.ds(0, size)],
        )

    for c in ORDER[:EARLY]:
        unpack(c)
        deposit(c)
        if c == ORDER[0]:
            pl.semaphore_wait(
                barrier, 2 + has_outer.astype(jnp.int32) + has_inner.astype(jnp.int32)
            )
        send_channel(c)
    for c in ORDER[EARLY:]:
        unpack(c)

    depth = lax.broadcasted_iota(jnp.int32, (width, 128), 0)
    lane = lax.broadcasted_iota(jnp.int32, (width, 128), 1)
    place = lane // 20
    odd = lane % 2 == 1
    mirror = jnp.where(place == 1, jnp.where(odd, width - 2, 1), jnp.where(odd, width - 1, 0))
    hit = (mirror == depth) & (place < 2)
    channel = (lane % 20) // 2
    select = jnp.concatenate(
        [jnp.where(hit & (channel == c), 1.0, 0.0).astype(jnp.bfloat16) for c in range(CHANNELS)],
        axis=0,
    )

    strip[...] = deposited(
        dot(high[...], select).astype(jnp.bfloat16), dot(low[...], select).astype(jnp.bfloat16)
    )
    to_outer = pltpu.make_async_remote_copy(
        src_ref=strip, dst_ref=strip_left, send_sem=band_send.at[0], recv_sem=band_recv.at[0],
        device_id={"rad": outer}, device_id_type=MESH,
    )
    to_inner = pltpu.make_async_remote_copy(
        src_ref=strip, dst_ref=strip_right, send_sem=band_send.at[1], recv_sem=band_recv.at[1],
        device_id={"rad": inner}, device_id_type=MESH,
    )

    @pl.when(has_outer)
    def _():
        to_outer.start()

    @pl.when(has_inner)
    def _():
        to_inner.start()

    for c in ORDER[EARLY:FIRST]:
        deposit(c)
        send_channel(c)
    for c in ORDER[FIRST:]:
        deposit(c)

    @pl.when(has_inner)
    def _():
        to_outer.wait_recv()

    @pl.when(jnp.logical_not(has_inner))
    def _():
        strip_left[...] = jnp.zeros_like(strip_left)

    @pl.when(has_outer)
    def _():
        to_inner.wait_recv()

    @pl.when(jnp.logical_not(has_outer))
    def _():
        strip_right[...] = jnp.zeros_like(strip_right)

    lane = lax.broadcasted_iota(jnp.int32, (LINES, 128), 1)
    edges = jnp.where(lane % 2 == 0, strip_right[...], strip_left[...])
    edge_out[0] = jnp.transpose(edges[LINES - SEND :])[:EDGES]
    edge_out[1] = jnp.transpose(edges[:SEND])[:EDGES]
    send(CHANNELS, edge_out.at[0], edge_left, edge_out.at[1], edge_right)

    for c in ORDER[FIRST:]:
        send_channel(c)

    def arrived(name):
        for copy in sends[name]:
            copy.wait_recv()

    arrived(CHANNELS)
    nothing = jnp.zeros((128 - EDGES, 128), jnp.float32)
    edges = jnp.concatenate(
        [
            edges[2 * H : 6 * H] + jnp.transpose(jnp.concatenate([edge_left[...], nothing], axis=0)),
            edges[6 * H : 8 * H],
            edges[8 * H : 12 * H] + jnp.transpose(jnp.concatenate([edge_right[...], nothing], axis=0)),
        ],
        axis=0,
    )
    lane = lax.broadcasted_iota(jnp.int32, (1, 128), 1)
    inside = jnp.where(lane == 0, has_inner.astype(jnp.float32), has_outer.astype(jnp.float32))

    def beside_in_band(value, edge):
        return (
            jnp.where(lane == 0, edge, pltpu.roll(value, 1, 1)),
            jnp.where(lane == 127, edge, pltpu.roll(value, 127, 1)),
        )

    radius = (width * n_rad + band * width + lane).astype(jnp.float32) + 0.5
    scale_az = 0.5 / (radius * (2.0 * math.pi / total_rows))
    recip = 1.0 / radius
    cell = lax.broadcasted_iota(jnp.int32, (CA * H, 1), 0) & (H - 1)

    def smooth(c):
        arrived(c)
        if c in WIDE:
            total = jnp.concatenate(
                [
                    part[c, 2 * H : 6 * H] + from_left[c],
                    part[c, 6 * H : 8 * H],
                    part[c, 8 * H : 12 * H] + from_right[c],
                ],
                axis=0,
            )
            edge = edges
        else:
            total = jnp.concatenate(
                [
                    part[c, 3 * H : 6 * H] + from_left[c, H:],
                    part[c, 6 * H : 8 * H],
                    part[c, 8 * H : 11 * H] + from_right[c, : 3 * H],
                ],
                axis=0,
            )
            edge = edges[H : H + CA * H]
        near = pltpu.roll(edge, 127 - 2 * c, 1)
        before, after = beside_in_band(total, near)
        result = 0.5 * total + 0.25 * (before + after)
        smoothed_ref[c] = center(result) if c in WIDE else result
        if c not in RADIAL:
            return result
        if c in WIDE:
            edge, near, total = center(edge), center(near), center(total)
        far = pltpu.roll(edge, 107 - 2 * c, 1)
        return result, (0.5 * near + 0.25 * (far + total)) * inside

    def grad_az(value):
        return (value[2 * H :] - value[: CA * H]) * scale_az

    def center(value):
        return value[H : H + CA * H]

    def grad_rad(value, edge):
        before, after = beside_in_band(value, edge)
        return (after - before) * 0.5

    def grad_height(value):
        below = jnp.where(cell == 0, 0.0, pltpu.roll(value, 1, 0))
        above = jnp.where(cell == H - 1, 0.0, pltpu.roll(value, CA * H - 1, 0))
        return (above - below) * 0.5

    value, edge = smooth(0)
    density, edge_density = 1.0 / (value + density_base), 1.0 / (edge + density_base)
    value, edge = smooth(1)
    value, edge = value * density, edge * edge_density
    middle = center(value)
    strain_ref[0] = grad_az(value)
    strain_ref[3] = grad_height(middle)
    strain_ref[4] = grad_rad(middle, edge) - middle * recip
    value, edge = smooth(2)
    value, edge = value * density, edge * edge_density
    middle = center(value)
    strain_ref[1] = grad_height(middle)
    strain_ref[3] = 0.5 * (strain_ref[3] + grad_az(value))
    strain_ref[5] = grad_rad(middle, edge)
    value, edge = smooth(3)
    value, edge = value * density, edge * edge_density
    middle = center(value)
    strain_ref[0] += middle * recip
    strain_ref[2] = grad_rad(middle, edge)
    strain_ref[4] = 0.5 * (strain_ref[4] + grad_az(value))
    strain_ref[5] = 0.5 * (strain_ref[5] + grad_height(middle))
    value = smooth(4)
    force_ref[0] = grad_az(value)
    force_ref[2] = -center(value) * recip
    value = smooth(7)
    force_ref[0] += grad_height(center(value))
    force_ref[1] = grad_az(value)
    value, edge = smooth(8)
    middle = center(value)
    force_ref[0] += grad_rad(middle, edge) + 2.0 * middle * recip
    force_ref[2] += grad_az(value)
    force_ref[1] += grad_height(smooth(5))
    middle, edge = smooth(6)
    force_ref[2] += grad_rad(middle, edge) + middle * recip
    middle, edge = smooth(9)
    force_ref[1] += grad_rad(middle, edge)
    force_ref[2] += grad_height(middle)

    for pair in sends.values():
        for copy in pair:
            copy.wait_send()

    @pl.when(has_outer)
    def _():
        to_outer.wait_send()

    @pl.when(has_inner)
    def _():
        to_inner.wait_send()


def store(smoothed, force, strain, smoothed_out, force_out, strain_out, sem):
    half = CHANNELS // 2
    copies = [
        pltpu.make_async_copy(source, target, sem.at[i])
        for i, (source, target) in enumerate(
            (
                (smoothed.at[pl.ds(0, half)], smoothed_out.at[pl.ds(0, half)]),
                (smoothed.at[pl.ds(half, half)], smoothed_out.at[pl.ds(half, half)]),
                (strain, strain_out),
                (force, force_out),
            )
        )
    ]
    for copy in copies:
        copy.start()
    for copy in copies:
        copy.wait()


def local(block_mass, block_flux, block_dest, block_count):
    n_az = lax.axis_size("az")
    n_rad = lax.axis_size("rad")
    slots, width = block_mass.shape[2:]
    cells = CA * H
    f32 = jnp.float32
    outs = pl.pallas_call(
        functools.partial(kernel, n_az, n_rad),
        out_shape=[pltpu.VMEM((k, cells, width), f32) for k in (CHANNELS, 3, 6)],
        in_specs=[
            pl.BlockSpec(memory_space=pltpu.SMEM),
            pl.BlockSpec(memory_space=pl.ANY),
            pl.BlockSpec(memory_space=pl.ANY),
            pl.BlockSpec(memory_space=pl.ANY),
        ],
        out_specs=[pl.BlockSpec(memory_space=pltpu.VMEM)] * 3,
        scratch_shapes=[
            pltpu.VMEM((1, slots), jnp.int32),
            pltpu.VMEM((CHANNELS, slots, width), f32),
            pltpu.VMEM((slots, CHANNELS * width), jnp.bfloat16),
            pltpu.VMEM((slots, CHANNELS * width), jnp.bfloat16),
            pltpu.VMEM((LINES, slots), jnp.bfloat16),
            pltpu.VMEM((CHANNELS, LINES, width), f32),
            pltpu.VMEM((CHANNELS, SEND, width), f32),
            pltpu.VMEM((CHANNELS, SEND, width), f32),
            pltpu.VMEM((LINES, 128), f32),
            pltpu.VMEM((LINES, 128), f32),
            pltpu.VMEM((LINES, 128), f32),
            pltpu.VMEM((2, EDGES, SEND), f32),
            pltpu.VMEM((EDGES, SEND), f32),
            pltpu.VMEM((EDGES, SEND), f32),
            pltpu.SemaphoreType.DMA((CHANNELS + 1,)),
            pltpu.SemaphoreType.DMA((2, CHANNELS + 1)),
            pltpu.SemaphoreType.DMA((2, CHANNELS + 1)),
            pltpu.SemaphoreType.DMA((2,)),
            pltpu.SemaphoreType.DMA((2,)),
        ],
        compiler_params=pltpu.CompilerParams(
            collective_id=0, has_side_effects=True, vmem_limit_bytes=56 * 1024 * 1024
        ),
    )(
        block_count,
        block_dest.reshape(1, slots),
        block_mass.reshape(slots, width),
        jnp.transpose(block_flux.reshape(slots, 9, width), (1, 0, 2)),
    )
    outs = pl.pallas_call(
        store,
        out_shape=[jax.ShapeDtypeStruct((k, cells, width), f32) for k in (CHANNELS, 3, 6)],
        in_specs=[pl.BlockSpec(memory_space=pltpu.VMEM)] * 3,
        out_specs=[pl.BlockSpec(memory_space=pltpu.HBM)] * 3,
        scratch_shapes=[pltpu.SemaphoreType.DMA((4,))],
        compiler_params=pltpu.CompilerParams(vmem_limit_bytes=8 * 1024 * 1024),
    )(*outs)
    return tuple(out.reshape(out.shape[0], CA, H, width) for out in outs)


def solution(mesh):
    return jax.shard_map(
        local,
        mesh=mesh,
        in_specs=(
            P("az", "rad", None, None),
            P("az", "rad", None, None, None),
            P("az", "rad", None),
            P("az", "rad"),
        ),
        out_specs=(
            P(None, "az", None, "rad"),
            P(None, "az", None, "rad"),
            P(None, "az", None, "rad"),
        ),
        check_vma=False,
    )
```
